256 devices in a mesh: src: 8 (over z_lo, y), tgt: 32 (over x, z_hi, core).
Axes of the slice: x: 4, y: 4, z: 8 (z_hi: 4, z_lo: 2; z = z_hi * 2 + z_lo), core: 2. Of those that a mesh axis runs over, the one named last changes fastest.
Arguments:
- source_feat: float32 [2048, 256], P(('src', 'tgt')), may hold values from -6 to 6
- target_feat: float32 [131072, 256], P('tgt'), may hold values from -6 to 6
- target_order: int32 [131072], P('tgt'), may hold values from 0 to 131071, as said below
- window_id: int32 [2048], replicated, may hold values from 0 to 80, as said below
- latent_query: float32 [8, 128], replicated, may hold values from -120 to 120
- patch_weight: float32 [64, 128], replicated, may hold values from -0.75 to 0.75
- patch_embed_bias: float32 [128], replicated, may hold values from -4 to 4
- key_weight: float32 [128, 128], replicated, may hold values from -0.5 to 0.5
- value_matrix: float32 [128, 128], replicated, may hold values from -0.5 to 0.5
- window_query: float32 [128, 128], replicated, may hold values from -4 to 4
- window_key: float32 [128, 128], replicated, may hold values from -0.5 to 0.5
- window_value: float32 [128, 128], replicated, may hold values from -0.5 to 0.5
- window_out: float32 [128, 128], replicated, may hold values from -0.5 to 0.5
- norm_gain: float32 [128], replicated, may hold values from 0.25 to 1.75
- up_weight: float32 [128, 512], replicated, may hold values from -0.5 to 0.5
- up_bias: float32 [512], replicated, may hold values from -4 to 4
- down_weight: float32 [512, 128], replicated, may hold values from -0.25 to 0.25
Outputs:
- cost_memory: float32 [2048, 8, 128], P(('src', 'tgt'))
The draws below stay inside these ranges and needn't reach their ends.
Inputs may be any that keep to these rules, and one draw needn't show every extreme that they name: `target_order`: each aligned block of 4096 entries holds every index of that block exactly once. `window_id`: source pixels are numbered row after row, 64 to a row; pixels with equal ids lie within one band of 256 consecutive pixels or within two neighbouring bands.
All inputs are finite; a program needn't handle non-finite values.
Results may differ from the reference program's by a relative error of at most 0.0003.
Values sent between devices are 32-bit elements; how exact they have to be, the bound alone decides.
A program may use at most 192 MiB of HBM per device.

```python
import math
import jax
import jax.numpy as jnp
from jax import lax

C = 256
D = 128
FF = 512
LATENTS = 8
PATCH = 64
IMG_W = 64
SRC_DEV = 256
T_DEV = 4096
SOURCES = 2048
TARGETS = 131072


def draw_target_order(key, part):
    key = jax.random.fold_in(key, 11)
    blocks = TARGETS // T_DEV
    keys = jax.random.split(key, blocks)
    perms = jax.vmap(lambda one: jax.random.permutation(one, T_DEV))(keys)
    starts = (jnp.arange(blocks, dtype=jnp.int32) * T_DEV)[:, None]
    return (perms.astype(jnp.int32) + starts).reshape(-1).astype(jnp.int32)


def draw_window_id(key, part):
    key = jax.random.fold_in(key, 12)
    row_key, col_key = jax.random.split(key)
    band_rows = SRC_DEV // IMG_W
    row_shift = jax.random.randint(row_key, (), 1, band_rows)
    col_shift = jax.random.randint(col_key, (), 1, 8)
    index = jnp.arange(SOURCES, dtype=jnp.int32)
    rows = index // IMG_W
    cols = index % IMG_W
    return ((rows + row_shift) // band_rows * (IMG_W // 8 + 1) + (cols + col_shift) // 8).astype(jnp.int32)


def draw_latent_query(key, part):
    key = jax.random.fold_in(key, 13)
    base_key = jax.random.fold_in(key, 0)
    base = jax.random.normal(base_key, (LATENTS, D), jnp.float32)
    return jnp.clip(base, -6.0, 6.0)


def draw_window_query(key, part):
    key = jax.random.fold_in(key, 14)
    base_key = jax.random.fold_in(key, 0)
    base = jax.random.normal(base_key, (D, D), jnp.float32) / math.sqrt(D)
    return jnp.clip(base, -4.0, 4.0)


def block_levels(own_key, dims, cuts, least, top_value):
    loudness, own = 1.0, jax.random.fold_in(own_key, 6)
    for position, shards_of in cuts:
        heights = jnp.exp(jax.random.uniform(jax.random.fold_in(own, position), (shards_of,), jnp.float32, least / len(cuts), top_value / len(cuts)))
        loudness = loudness * jnp.repeat(heights, dims[position] // shards_of).reshape([-1 if axis == position else 1 for axis in range(len(dims))])
    return loudness


def centred(rng, dims, scale, most, shards=(), kind=jnp.bfloat16):
    result = scale * jax.random.normal(rng, dims, jnp.float32)
    if shards:
        result = result * block_levels(rng, dims, shards, -0.22, 0.18)
    return jnp.clip(result, -most, most).astype(kind)


def setup_inputs(seed: int = 0) -> dict:
    key_list = jax.random.split(jax.random.key(seed), 18)
    return {
        "source_feat": centred(key_list[0], (SOURCES, C), 1.0, 6.0, ((0, 256),), jnp.float32),
        "target_feat": centred(key_list[1], (TARGETS, C), 1.0, 6.0, ((0, 32),), jnp.float32),
        "target_order": draw_target_order(jax.random.fold_in(key_list[17], 71), 0),
        "window_id": draw_window_id(jax.random.fold_in(key_list[17], 71), 0),
        "latent_query": draw_latent_query(jax.random.fold_in(key_list[17], 71), 0),
        "patch_weight": centred(key_list[5], (PATCH, D), PATCH ** -0.5, 0.75, (), jnp.float32),
        "patch_embed_bias": centred(key_list[6], (D,), 0.7, 4.0, (), jnp.float32),
        "key_weight": centred(key_list[7], (D, D), D ** -0.5, 0.5, (), jnp.float32),
        "value_matrix": centred(key_list[8], (D, D), D ** -0.5, 0.5, (), jnp.float32),
        "window_query": draw_window_query(jax.random.fold_in(key_list[17], 71), 0),
        "window_key": centred(key_list[10], (D, D), D ** -0.5, 0.5, (), jnp.float32),
        "window_value": centred(key_list[11], (D, D), D ** -0.5, 0.5, (), jnp.float32),
        "window_out": centred(key_list[12], (D, D), D ** -0.5, 0.5, (), jnp.float32),
        "norm_gain": jnp.clip(1.0 + 0.15 * jax.random.normal(key_list[13], (D,), jnp.float32), 0.25, 1.75),
        "up_weight": centred(key_list[14], (D, FF), D ** -0.5, 0.5, (), jnp.float32),
        "up_bias": centred(key_list[15], (FF,), 0.7, 4.0, (), jnp.float32),
        "down_weight": centred(key_list[16], (FF, D), FF ** -0.5, 0.25, (), jnp.float32),
    }


HIGH_PRECISION = lax.Precision.HIGHEST

def reference(source_feat, target_feat, target_order, window_id, latent_query, patch_weight, patch_embed_bias, key_weight, value_matrix, window_query, window_key, window_value, window_out, norm_gain, up_weight, up_bias, down_weight):
    ordered = jnp.take(target_feat, target_order, axis=0)
    key_query = jnp.dot(key_weight, latent_query.T, precision=HIGH_PRECISION) / math.sqrt(D)

    def latent_block(rows):
        cost = jnp.dot(rows, ordered.T, precision=HIGH_PRECISION) / math.sqrt(C)
        patches = cost.reshape(rows.shape[0], TARGETS // PATCH, PATCH)
        embed_patches = jnp.einsum('bpq,qd->bpd', patches, patch_weight, precision=HIGH_PRECISION) + patch_embed_bias
        score = jnp.einsum('bpd,dk->bkp', embed_patches, key_query, precision=HIGH_PRECISION)
        attend_windows = jax.nn.softmax(score, axis=-1)
        summed_rows = jnp.einsum('jws,jsy->jwy', attend_windows, embed_patches, precision=HIGH_PRECISION)
        return jnp.einsum('xso,om->xsm', summed_rows, value_matrix, precision=HIGH_PRECISION)
    latent = lax.map(latent_block, source_feat.reshape(SOURCES // 128, 128, C)).reshape(SOURCES, LATENTS, D)
    query = jnp.einsum('skd,de->kse', latent, window_query, precision=HIGH_PRECISION)
    keys = jnp.einsum('skd,de->kse', latent, window_key, precision=HIGH_PRECISION)
    values = jnp.einsum('skd,de->kse', latent, window_value, precision=HIGH_PRECISION)
    same = window_id[:, None] == window_id[None, :]

    def one_slot(operands):
        slot_query, slot_keys, slot_values = operands
        scores = jnp.dot(slot_query, slot_keys.T, precision=HIGH_PRECISION) / math.sqrt(D)
        scores = jnp.where(same, scores, -jnp.inf)
        return jnp.dot(jax.nn.softmax(scores, axis=-1), slot_values, precision=HIGH_PRECISION)
    mixed = lax.map(one_slot, (query, keys, values))
    resid = latent + jnp.einsum('kse,ed->skd', mixed, window_out, precision=HIGH_PRECISION)
    center = lax.optimization_barrier(jnp.mean(resid, axis=-1, keepdims=True))
    spread_values = lax.optimization_barrier(jnp.mean((resid - center) ** 2, axis=-1, keepdims=True))
    normed = (resid - center) / jnp.sqrt(spread_values + 1e-05) * norm_gain
    hidden = jax.nn.gelu(jnp.einsum('skd,df->skf', normed, up_weight, precision=HIGH_PRECISION) + up_bias)
    return resid + jnp.einsum('skf,fd->skd', hidden, down_weight, precision=HIGH_PRECISION)
```

```python
import functools
import math

import jax
import jax.numpy as jnp
from jax import lax
from jax.experimental import pallas as pl
from jax.experimental.pallas import tpu as pltpu
from jax.sharding import PartitionSpec as P

HI = lax.Precision.HIGHEST
MESH = pl.DeviceIdType.MESH
F32 = jnp.float32

NX, NH, NC = 4, 4, 2
BAND = 256
C = 256
D = 128
K = 8
PATCH = 64
TARGETS = 4096
PATCHES = TARGETS // PATCH
ROWS = 8
QC = PATCH // NH
PIX = BAND // NH


def nn(a, b):
    return lax.dot_general(a, b, (((1,), (0,)), ((), ())), precision=HI, preferred_element_type=F32)


def nt(a, b):
    return lax.dot_general(a, b, (((1,), (1,)), ((), ())), precision=HI, preferred_element_type=F32)


def kernel(
    bands, tgt, src_h, order_h, wid_h, lq_h, pw_h, pb_h, kw_h, vm_h, wq_h, wk_h, wv_h, wo_h, gain_h, up_h, upb_h, down_h,
    out,
    src, order, wid, lq, pw, pb, kw, vm, wq, wk, wv, wo, gain, up, upb, down,
    raw, addr_v, addr, ordered, sbuf, gmat, wts, cost,
    st, st_core, st_x, st_h, zc, core_in, zx, x_in, zh, h_in, zt, fin_out, fin_in,
    wsem, tsem, asem, ssem, rsem,
):
    band = lax.axis_index("src")
    t = lax.axis_index("tgt")
    x = t // (NH * NC)
    h = (t // NC) % NH
    c = t % NC
    mine = c * NX + x

    def tid(xx, hh, cc):
        return (xx * NH + hh) * NC + cc

    sib = (band, tid(x, h, 1 - c))
    xs = [(x + d) % NX for d in range(1, NX)]
    hs = [(h + d) % NH for d in range(1, NH)]
    x_peer = [(band, tid(xx, h, c)) for xx in xs]
    h_peer = [(band, tid(x, hh, c)) for hh in hs]
    o_peer = [(band, tid((x + d) % NX, h, 1 - c)) for d in range(1, NX)]
    up_band = (band + 1) % bands
    down_band = (band + bands - 1) % bands
    y_peer = [(up_band, t), (down_band, t)]

    weights = list(zip(
        (src_h, order_h, wid_h, lq_h, pw_h, pb_h, kw_h, vm_h, wq_h, wk_h, wv_h, wo_h, gain_h, up_h, upb_h, down_h),
        (src, order, wid, lq, pw, pb, kw, vm, wq, wk, wv, wo, gain, up, upb, down),
    ))
    loads = [pltpu.make_async_copy(a, b, wsem.at[i]) for i, (a, b) in enumerate(weights)]
    for one in loads[:2]:
        one.start()
    load_target = pltpu.make_async_copy(tgt, raw.at[pl.ds(8, 2 * TARGETS)], tsem)
    load_target.start()
    for one in loads[2:]:
        one.start()

    barrier = pltpu.get_barrier_semaphore()
    partners = [sib] + x_peer + o_peer + h_peer + y_peer
    for who in partners:
        pl.semaphore_signal(barrier, inc=1, device_id=who, device_id_type=MESH)

    loads[0].wait()
    loads[1].wait()
    ids = order[...] & (TARGETS - 1)
    addr_v[...] = (ids >> 3) * 16 + (ids & 7)
    to_smem = pltpu.make_async_copy(addr_v, addr, asem)
    to_smem.start()

    count = [0]
    sends = []

    def send(a, b, who):
        n = count[0]
        count[0] = n + 1
        copy = pltpu.make_async_remote_copy(
            src_ref=a, dst_ref=b, send_sem=ssem.at[n], recv_sem=rsem.at[n], device_id=who, device_id_type=MESH
        )
        copy.start()
        sends.append(copy)
        return copy

    pl.semaphore_wait(barrier, len(partners))

    slot = pl.multiple_of(c * (NX * ROWS) + x * ROWS, ROWS)
    half = pl.multiple_of(c * (NX * ROWS), NX * ROWS)
    sbuf[h, pl.ds(slot, ROWS), :] = src[...] * (1.0 / math.sqrt(C))
    own = sbuf.at[h, pl.ds(slot, ROWS)]
    s1 = [send(own, own, who) for who in h_peer]

    for one in loads[2:]:
        one.wait()
    scale = 1.0 / math.sqrt(D)
    kq = nt(lq[...], kw[...]) * scale
    w2 = nt(kq, pw[...])
    bias_k = jnp.sum(kq * pb[...], axis=1, keepdims=True)
    w2x4 = jnp.concatenate([w2] * 4, axis=1)
    patch_of = lax.broadcasted_iota(jnp.int32, (K, 4 * PATCH), 1) // PATCH
    spread = jnp.concatenate([jnp.where(patch_of == i, w2x4, 0.0) for i in range(4)], axis=0)

    load_target.wait()
    to_smem.wait()
    sub = lax.broadcasted_iota(jnp.int32, (8, 128), 0)
    masks = [sub == i for i in range(8)]

    def gather_patch(p, _):
        for g in range(8):
            at = [addr[p // 2, (p % 2) * 64 + g * 8 + i] for i in range(8)]
            for lane in range(2):
                rows = [raw[pl.ds(at[i] + 8 + 8 * lane - i, 8), :] for i in range(8)]
                total = rows[0]
                for i in range(1, 8):
                    total = jnp.where(masks[i], rows[i], total)
                ordered[p, g, :, lane * 128:lane * 128 + 128] = total
        return 0

    def gather(first, last):
        lax.fori_loop(first, last, gather_patch, 0)

    gather(0, 16)
    for one in s1:
        one.wait_recv()
    col = sbuf.at[:, pl.ds(slot, ROWS)]
    s2 = [send(col, col, who) for who in x_peer]
    gather(16, 40)
    for one in s2:
        one.wait_recv()
    part = sbuf.at[:, pl.ds(half, NX * ROWS)]
    s3 = send(part, part, sib)
    gather(40, 64)

    def score_weights(g, _):
        block = ordered[pl.ds(g * 4, 4)].reshape(4 * PATCH, C)
        gmat[pl.ds(pl.multiple_of(g * 32, 32), 32), :] = nn(spread, block)
        return 0

    lax.fori_loop(0, PATCHES // 4, score_weights, 0)
    s3.wait_recv()

    rows = sbuf[...].reshape(BAND, C)
    score = nt(gmat[...], rows).reshape(PATCHES, K, BAND) + bias_k[None]
    peak = jnp.max(score, axis=0)
    weight = jnp.exp(score - peak[None])
    wts[...] = weight
    st[0] = peak
    st[1] = jnp.sum(weight, axis=0)
    m1 = send(st, st_core, sib)

    def cost_chunk(q, _):
        block = ordered[:, pl.ds(q * 2, 2)].reshape(PATCHES * QC, C)
        cost[q] = nt(block, sbuf[...].reshape(BAND, C)).reshape(PATCHES, QC, BAND)
        return 0

    def join(values):
        top = functools.reduce(jnp.maximum, [a for a, _ in values])
        return top, sum(b * jnp.exp(a - top) for a, b in values)

    lax.fori_loop(0, 1, cost_chunk, 0)
    m1.wait_recv()
    top, tot = join([(peak, st[1]), (st_core[0], st_core[1])])
    st_x[NX - 1, 0] = top
    st_x[NX - 1, 1] = tot
    m2 = [send(st_x.at[NX - 1], st_x.at[i], who) for i, who in enumerate(x_peer)]
    lax.fori_loop(1, 3, cost_chunk, 0)
    for one in m2:
        one.wait_recv()
    top, tot = join([(st_x[i, 0], st_x[i, 1]) for i in range(NX)])
    st_h[NH - 1, 0] = top
    st_h[NH - 1, 1] = tot
    m3 = [send(st_h.at[NH - 1], st_h.at[i], who) for i, who in enumerate(h_peer)]
    lax.fori_loop(3, 4, cost_chunk, 0)

    pv = nn(pw[...], vm[...])
    bv = nn(pb[...], vm[...])
    pk = nn(pv, wk[...])
    bk = nn(bv, wk[...])
    pq = nn(pv, wq[...]) * scale
    bq = nn(bv, wq[...]) * scale
    val = nn(wv[...], wo[...])
    pval = nn(pv, val)
    bval = nn(bv, val)
    pk_all = jnp.concatenate([pk, jnp.broadcast_to(bk, (PATCH, D))], axis=0)
    wq_all = nt(pq, pk_all)
    cq_all = nt(bq, pk_all)

    nat = lax.broadcasted_iota(jnp.int32, (BAND, BAND), 0)
    pos = lax.broadcasted_iota(jnp.int32, (BAND, BAND), 1)
    ph, pc, px, pr = pos // 64, (pos // 32) % 2, (pos // 8) % 4, pos % 8
    perm = jnp.where(nat == px * 64 + ph * 16 + pc * 8 + pr, 1.0, 0.0).astype(F32)
    id_rows = []
    for b in (down_band, band, up_band):
        two = [wid[pl.ds(2 * b + i, 1), :].astype(F32) for i in range(2)]
        id_rows.append(nn(jnp.broadcast_to(jnp.concatenate(two, axis=1), (8, BAND)), perm)[0:1])
    picked = lax.broadcasted_iota(jnp.int32, (PIX, BAND), 1) == lax.broadcasted_iota(jnp.int32, (PIX, BAND), 0) + h * PIX
    q_ids = jnp.sum(jnp.where(picked, id_rows[1], 0.0), axis=1, keepdims=True)
    choose = jnp.where(picked, 1.0, 0.0).astype(F32)

    for one in m3:
        one.wait_recv()
    top, tot = join([(st_h[i, 0], st_h[i, 1]) for i in range(NH)])
    factor = jnp.exp(st[0] - top) / tot

    def chunk_of(i):
        return (h + 1 + i) % NH

    def sums(i):
        q = chunk_of(i)
        for lane in range(2):
            cut = slice(lane * 128, lane * 128 + 128)

            def step(p, acc):
                both = cost[q, p, :, cut]
                new = []
                for k in range(K):
                    w = jnp.broadcast_to(wts[p, k:k + 1, cut], (8, 128))
                    new.append(acc[2 * k] + w * both[0:8])
                    new.append(acc[2 * k + 1] + w * both[8:16])
                return tuple(new)

            acc = lax.fori_loop(0, PATCHES, step, tuple(jnp.zeros((8, 128), F32) for _ in range(2 * K)), unroll=8)
            for k in range(K):
                f = factor[k:k + 1, cut]
                zc[i, k, 0:8, cut] = acc[2 * k] * f
                zc[i, k, 8:16, cut] = acc[2 * k + 1] * f
        return send(zc.at[i, pl.ds((1 - c) * NX, NX)], core_in.at[i], sib)

    def over_x(i, came):
        came.wait_recv()
        zx[i] = zc[i, pl.ds(c * NX, NX)] + core_in[i]
        return [send(zx.at[i, xx], x_in.at[i, j], who) for j, (xx, who) in enumerate(zip(xs, x_peer))]

    def over_h(i, came):
        for one in came:
            one.wait_recv()
        zh[i] = zx[i, x] + x_in[i, 0] + x_in[i, 1] + x_in[i, 2]
        if i < NH - 1:
            return send(zh.at[i], h_in.at[i], h_peer[i])

    a0 = sums(0)
    a1 = sums(1)
    b0 = over_x(0, a0)
    a2 = sums(2)
    b1 = over_x(1, a1)
    d0 = over_h(0, b0)
    a3 = sums(3)
    b2 = over_x(2, a2)
    d1 = over_h(1, b1)
    b3 = over_x(3, a3)
    d2 = over_h(2, b2)
    over_h(3, b3)
    for one in (d0, d1, d2):
        one.wait_recv()
    q_rows = pl.ds(pl.multiple_of(h * QC, QC), QC)
    zt[1, q_rows, :] = zh[NH - 1] + h_in[0] + h_in[1] + h_in[2]

    def to_bands(rows):
        return [send(zt.at[1, rows], zt.at[0, rows], y_peer[0]), send(zt.at[1, rows], zt.at[2, rows], y_peer[1])]

    e = [send(zt.at[1, q_rows], zt.at[1, q_rows], who) for who in h_peer]
    f = to_bands(q_rows)
    for d in range(1, NH):
        e[d - 1].wait_recv()
        f += to_bands(pl.ds(pl.multiple_of(((h + NH - d) % NH) * QC, QC), QC))

    zq = nt(choose, zt[1])
    qa = nn(zq, wq_all) + cq_all
    qz = qa[:, 0:PATCH]
    qb = qa[:, PATCH:PATCH + 1]
    for one in f:
        one.wait_recv()
    logits = jnp.concatenate([nn(qz, zt[b]) for b in range(3)], axis=1) + qb
    same = q_ids == jnp.concatenate(id_rows, axis=1)
    logits = jnp.where(same, logits, -jnp.inf)
    attend = jnp.exp(logits - jnp.max(logits, axis=1, keepdims=True))
    attend = attend / jnp.sum(attend, axis=1, keepdims=True)
    zmix = sum(nt(attend[:, b * BAND:(b + 1) * BAND], zt[b]) for b in range(3))
    resid = (nn(zq, pv) + bv) + (nn(zmix, pval) + bval)
    center = jnp.mean(resid, axis=-1, keepdims=True)
    var = jnp.mean((resid - center) ** 2, axis=-1, keepdims=True)
    normed = (resid - center) / jnp.sqrt(var + 1e-05) * gain[...]
    hidden = jax.nn.gelu(nn(normed, up[...]) + upb[...])
    fin_out[...] = resid + nn(hidden, down[...])

    g = []
    for d in range(1, NX):
        rows = pl.ds(pl.multiple_of((c * NX + xs[d - 1]) * ROWS, ROWS), ROWS)
        g.append(send(fin_out.at[rows], fin_in.at[mine], x_peer[d - 1]))
    for d in range(NX):
        rows = pl.ds(pl.multiple_of(((1 - c) * NX + (x + d) % NX) * ROWS, ROWS), ROWS)
        g.append(send(fin_out.at[rows], fin_in.at[mine], sib if d == 0 else o_peer[d - 1]))
    fin_in[mine] = fin_out[pl.ds(pl.multiple_of(mine * ROWS, ROWS), ROWS)]
    for one in g:
        one.wait_recv()
    for k in range(K):
        out[:, k, :] = fin_in[k]
    for one in sends:
        one.wait_send()


COPIES = 90


def local(
    source_feat, target_feat, target_order, window_id, latent_query, patch_weight, patch_embed_bias, key_weight,
    value_matrix, window_query, window_key, window_value, window_out, norm_gain, up_weight, up_bias, down_weight,
):
    bands = lax.axis_size("src")
    tiles = target_feat.reshape(TARGETS // 8, 8, 2, 128).transpose(0, 2, 1, 3).reshape(2 * TARGETS, 128)
    params = (
        source_feat, target_order.reshape(32, 128), window_id.reshape(16, 128),
        latent_query, patch_weight, patch_embed_bias.reshape(1, -1), key_weight, value_matrix, window_query, window_key,
        window_value, window_out, norm_gain.reshape(1, -1), up_weight, up_bias.reshape(1, -1), down_weight,
    )
    vmem = pl.BlockSpec(memory_space=pltpu.VMEM)
    hbm = pl.BlockSpec(memory_space=pl.ANY)
    scratch = [pltpu.VMEM(p.shape, p.dtype) for p in params]
    scratch += [
        pltpu.VMEM((2 * TARGETS + 16, 128), F32),
        pltpu.VMEM((32, 128), jnp.int32),
        pltpu.SMEM((32, 128), jnp.int32),
        pltpu.VMEM((PATCHES, 8, 8, C), F32),
        pltpu.VMEM((NH, PIX, C), F32),
        pltpu.VMEM((PATCHES * K, C), F32),
        pltpu.VMEM((PATCHES, K, BAND), F32),
        pltpu.VMEM((NH, PATCHES, QC, BAND), F32),
        pltpu.VMEM((2, K, BAND), F32),
        pltpu.VMEM((2, K, BAND), F32),
        pltpu.VMEM((NX, 2, K, BAND), F32),
        pltpu.VMEM((NH, 2, K, BAND), F32),
        pltpu.VMEM((NH, K, QC, BAND), F32),
        pltpu.VMEM((NH, NX, QC, BAND), F32),
        pltpu.VMEM((NH, NX, QC, BAND), F32),
        pltpu.VMEM((NH, NX - 1, QC, BAND), F32),
        pltpu.VMEM((NH, QC, BAND), F32),
        pltpu.VMEM((NH - 1, QC, BAND), F32),
        pltpu.VMEM((3, PATCH, BAND), F32),
        pltpu.VMEM((PIX, D), F32),
        pltpu.VMEM((K, ROWS, D), F32),
        pltpu.SemaphoreType.DMA((len(params),)),
        pltpu.SemaphoreType.DMA,
        pltpu.SemaphoreType.DMA,
        pltpu.SemaphoreType.DMA((COPIES,)),
        pltpu.SemaphoreType.DMA((COPIES,)),
    ]
    return pl.pallas_call(
        functools.partial(kernel, bands),
        out_shape=jax.ShapeDtypeStruct((ROWS, K, D), F32),
        in_specs=[hbm] * (1 + len(params)),
        out_specs=vmem,
        scratch_shapes=scratch,
        compiler_params=pltpu.CompilerParams(
            collective_id=0, has_side_effects=True, vmem_limit_bytes=60 * 1024 * 1024
        ),
        name="encode",
    )(tiles, *params)


def solution(mesh):
    placed = (P(("src", "tgt"), None), P("tgt", None), P("tgt")) + (P(),) * 14
    return jax.shard_map(
        local, mesh=mesh, in_specs=placed, out_specs=P(("src", "tgt"), None, None), check_vma=False
    )
```

```python
import functools
import math

import jax
import jax.numpy as jnp
from jax import lax
from jax.experimental import pallas as pl
from jax.experimental.pallas import tpu as pltpu
from jax.sharding import PartitionSpec as P

HI = lax.Precision.HIGHEST
MESH = pl.DeviceIdType.MESH
F32 = jnp.float32

NX, NH, NC = 4, 4, 2
BAND = 256
C = 256
D = 128
K = 8
PATCH = 64
TARGETS = 4096
PATCHES = TARGETS // PATCH
ROWS = 8
PARTS = 4
QC = PATCH // PARTS
PIX = BAND // NH


def nn(a, b):
    return lax.dot_general(a, b, (((1,), (0,)), ((), ())), precision=HI, preferred_element_type=F32)


def nt16(a, b):
    return lax.dot_general(a, b, (((1,), (1,)), ((), ())), preferred_element_type=F32)


def halves(a):
    high = a.astype(jnp.bfloat16)
    return high, (a - high.astype(F32)).astype(jnp.bfloat16)


def nt(a, b):
    return lax.dot_general(a, b, (((1,), (1,)), ((), ())), precision=HI, preferred_element_type=F32)


def kernel(
    bands, tgt, src_h, order_h, wid_h, lq_h, pw_h, pb_h, kw_h, vm_h, wq_h, wk_h, wv_h, wo_h, gain_h, up_h, upb_h, down_h,
    out,
    src, order, wid, lq, pw, pb, kw, vm, wq, wk, wv, wo, gain, up, upb, down,
    raw, addr_v, addr, ordered, sbuf, scat, gmat, wts, cost,
    st, st_core, fac, st_x, st_h, zc, core_in, zx, x_in, zh, h_in, zt, fin_out, fin_in,
    wsem, tsem, asem, ssem, rsem,
):
    band = lax.axis_index("src")
    t = lax.axis_index("tgt")
    x = t // (NH * NC)
    h = (t // NC) % NH
    c = t % NC
    mine = c * NX + x

    def tid(xx, hh, cc):
        return (xx * NH + hh) * NC + cc

    sib = (band, tid(x, h, 1 - c))
    xs = [(x + d) % NX for d in range(1, NX)]
    hs = [(h + d) % NH for d in range(1, NH)]
    x_peer = [(band, tid(xx, h, c)) for xx in xs]
    h_peer = [(band, tid(x, hh, c)) for hh in hs]
    o_peer = [(band, tid((x + d) % NX, h, 1 - c)) for d in range(1, NX)]
    up_band = (band + 1) % bands
    down_band = (band + bands - 1) % bands
    y_peer = [(up_band, t), (down_band, t)]

    weights = list(zip(
        (src_h, order_h, wid_h, lq_h, pw_h, pb_h, kw_h, vm_h, wq_h, wk_h, wv_h, wo_h, gain_h, up_h, upb_h, down_h),
        (src, order, wid, lq, pw, pb, kw, vm, wq, wk, wv, wo, gain, up, upb, down),
    ))
    loads = [pltpu.make_async_copy(a, b, wsem.at[i]) for i, (a, b) in enumerate(weights)]
    for one in loads[:2]:
        one.start()
    load_target = pltpu.make_async_copy(tgt, raw.at[pl.ds(8, 2 * TARGETS)], tsem)
    load_target.start()
    for one in loads[2:]:
        one.start()

    barrier = pltpu.get_barrier_semaphore()
    partners = h_peer + y_peer + x_peer + o_peer + [sib]
    for who in partners:
        pl.semaphore_signal(barrier, inc=1, device_id=who, device_id_type=MESH)

    loads[0].wait()
    loads[1].wait()
    ids = order[...] & (TARGETS - 1)
    addr_v[...] = (ids >> 3) * 16 + (ids & 7)
    to_smem = pltpu.make_async_copy(addr_v, addr, asem)
    to_smem.start()

    count = [0]
    sends = []

    def send(a, b, who):
        n = count[0]
        count[0] = n + 1
        copy = pltpu.make_async_remote_copy(
            src_ref=a, dst_ref=b, send_sem=ssem.at[n], recv_sem=rsem.at[n], device_id=who, device_id_type=MESH
        )
        copy.start()
        sends.append(copy)
        return copy

    slot = pl.multiple_of(c * (NX * ROWS) + x * ROWS, ROWS)
    half = pl.multiple_of(c * (NX * ROWS), NX * ROWS)
    sbuf[h, pl.ds(slot, ROWS), :] = src[...] * (1.0 / math.sqrt(C))
    pl.semaphore_wait(barrier, len(partners))
    own = sbuf.at[h, pl.ds(slot, ROWS)]
    s1 = [send(own, own, who) for who in h_peer]

    load_target.wait()
    to_smem.wait()
    sub = lax.broadcasted_iota(jnp.int32, (8, 128), 0)
    masks = [sub == i for i in range(8)]

    def gather_pair(r, _):
        for g in range(16):
            p = 2 * r + g // 8
            at = [addr[r, g * 8 + i] for i in range(8)]
            for lane in range(2):
                cols = slice(lane * 128, lane * 128 + 128)
                rows = [raw[pl.ds(at[i] + 8 + 8 * lane - i, 8), :] for i in range(8)]
                total = rows[0]
                for i in range(1, 8):
                    total = jnp.where(masks[i], rows[i], total)
                ordered[p, g % 8, :, cols] = total
        return 0

    def gather(first, last):
        lax.fori_loop(first, last, gather_pair, 0)

    gather(0, 20)
    for one in s1:
        one.wait_recv()
    col = sbuf.at[:, pl.ds(slot, ROWS)]
    s2 = [send(col, col, who) for who in x_peer]
    gather(20, 32)
    for one in loads[2:]:
        one.wait()
    scale = 1.0 / math.sqrt(D)
    kq = nt(lq[...], kw[...]) * scale
    w2 = nt(kq, pw[...])
    bias_k = jnp.sum(kq * pb[...], axis=1, keepdims=True)
    w2x4 = jnp.concatenate([w2] * 4, axis=1)
    patch_of = lax.broadcasted_iota(jnp.int32, (K, 4 * PATCH), 1) // PATCH
    spread = jnp.concatenate([jnp.where(patch_of == i, w2x4, 0.0) for i in range(4)], axis=0)


    def score_weights(g, _):
        block = ordered[pl.ds(g * 4, 4)].reshape(4 * PATCH, C)
        gmat[pl.ds(pl.multiple_of(g * 32, 32), 32), :] = nn(spread, block)
        return 0

    lax.fori_loop(0, PATCHES // 4, score_weights, 0, unroll=True)
    for one in s2:
        one.wait_recv()
    part = sbuf.at[:, pl.ds(half, NX * ROWS)]
    s3 = send(part, part, sib)
    s3.wait_recv()

    score = nt(gmat[...], sbuf[...].reshape(BAND, C)).reshape(PATCHES, K, BAND) + bias_k[None]
    peak = jnp.max(score, axis=0)
    weight = jnp.exp(score - peak[None])
    wts[...] = weight
    total = jnp.sum(weight, axis=0)
    st[0] = peak
    st[1] = total
    m1 = send(st, st_core, sib)

    shigh, slow = halves(sbuf[...].reshape(BAND, C))
    scat[:, 0:C] = shigh
    scat[:, C:2 * C] = slow
    scat[:, 2 * C:3 * C] = shigh

    def cost_chunk(q, _):
        block = ordered[:, pl.ds(q * (QC // 8), QC // 8)].reshape(PATCHES * QC, C)
        a, b = halves(block)
        part = nt16(jnp.concatenate([a, a, b], axis=1), scat[...])
        cost[q] = part.reshape(PATCHES, QC, BAND)
        return 0

    def join(values):
        top = functools.reduce(jnp.maximum, [a for a, _ in values])
        scales = [jnp.exp(a - top) for a, _ in values]
        return top, sum(b * f for (_, b), f in zip(values, scales)), scales

    lax.fori_loop(0, PARTS, cost_chunk, 0)
    m1.wait_recv()
    top, tot, scales = join([(st[0], st[1]), (st_core[0], st_core[1])])
    fac[0] = scales[0]
    fac[1] = scales[1]
    for k in range(K):
        st_x[k, 0:1, :] = top[k:k + 1]
        st_x[k, 1:2, :] = tot[k:k + 1]
    m2 = [send(st_x.at[c * NX + xx], st_x.at[K + i], who) for i, (xx, who) in enumerate(zip(xs, x_peer))]

    def sums(i):
        for lane in range(2):
            cols = slice(lane * 128, lane * 128 + 128)

            def step(p, acc):
                rows = [cost[i, p, g * 8:g * 8 + 8, cols] for g in range(QC // 8)]
                new = []
                for k in range(K):
                    w = jnp.broadcast_to(wts[p, k:k + 1, cols], (8, 128))
                    new.extend(acc[k * len(rows) + g] + w * one for g, one in enumerate(rows))
                return tuple(new)

            zero = tuple(jnp.zeros((8, 128), F32) for _ in range(QC // 8 * K))
            acc = lax.fori_loop(0, PATCHES, step, zero, unroll=8)
            for k in range(K):
                for g in range(QC // 8):
                    zc[i, k, g * 8:g * 8 + 8, cols] = acc[k * (QC // 8) + g]
        return send(zc.at[i, pl.ds((1 - c) * NX, NX)], core_in.at[i], sib)

    def over_x(i, came):
        came.wait_recv()
        for j in range(NX):
            k = c * NX + j
            zx[i, j] = zc[i, k] * fac[0, pl.ds(k, 1), :] + core_in[i, j] * fac[1, pl.ds(k, 1), :]
        return [send(zx.at[i, xx], x_in.at[i, j], who) for j, (xx, who) in enumerate(zip(xs, x_peer))]

    def x_stats():
        for one in m2:
            one.wait_recv()
        top, tot, scales = join([(st_x[i, 0:1, :], st_x[i, 1:2, :]) for i in (mine, K, K + 1, K + 2)])
        st_h[0, 0:1, :] = top
        st_h[0, 1:2, :] = tot
        return [send(st_h.at[0], st_h.at[1 + i], who) for i, who in enumerate(h_peer)], scales

    core = [sums(0)]
    over = []
    for i in range(1, PARTS):
        core.append(sums(i))
        over.append(over_x(i - 1, core[i - 1]))
    over.append(over_x(PARTS - 1, core[PARTS - 1]))
    m3, x_scales = x_stats()
    pv = nn(pw[...], vm[...])
    bv = nn(pb[...], vm[...])
    pk = nn(pv, wk[...])
    bk = nn(bv, wk[...])
    pq = nn(pv, wq[...]) * scale
    bq = nn(bv, wq[...]) * scale
    val = nn(wv[...], wo[...])
    pval = nn(pv, val)
    bval = nn(bv, val)
    pk_all = jnp.concatenate([pk, jnp.broadcast_to(bk, (PATCH, D))], axis=0)
    wq_all = nt(pq, pk_all)
    cq_all = nt(bq, pk_all)

    nat = lax.broadcasted_iota(jnp.int32, (BAND, BAND), 0)
    pos = lax.broadcasted_iota(jnp.int32, (BAND, BAND), 1)
    ph, pc, px, pr = pos // 64, (pos // 32) % 2, (pos // 8) % 4, pos % 8
    perm = jnp.where(nat == px * 64 + ph * 16 + pc * 8 + pr, 1.0, 0.0).astype(F32)
    id_rows = []
    for b in (down_band, band, up_band):
        two = [wid[pl.ds(2 * b + i, 1), :].astype(F32) for i in range(2)]
        id_rows.append(nn(jnp.broadcast_to(jnp.concatenate(two, axis=1), (8, BAND)), perm)[0:1])
    picked = lax.broadcasted_iota(jnp.int32, (PIX, BAND), 1) == lax.broadcasted_iota(jnp.int32, (PIX, BAND), 0) + h * PIX
    q_ids = jnp.sum(jnp.where(picked, id_rows[1], 0.0), axis=1, keepdims=True)
    choose = jnp.where(picked, 1.0, 0.0).astype(F32)


    def over_h(i, came):
        for one in came:
            one.wait_recv()
        total = zx[i, x] * x_scales[0]
        for j in range(NX - 1):
            total = total + x_in[i, j] * x_scales[1 + j]
        zh[i] = total
        return [send(zh.at[i], h_in.at[i, j], who) for j, who in enumerate(h_peer)]

    d = [over_h(i, came) for i, came in enumerate(over)]
    for one in m3:
        one.wait_recv()
    _, tot, h_scales = join([(st_h[i, 0:1, :], st_h[i, 1:2, :]) for i in range(NH)])
    inverse = 1.0 / tot
    h_scales = [f * inverse for f in h_scales]

    def to_bands(i):
        for one in d[i]:
            one.wait_recv()
        total = zh[i] * h_scales[0]
        for j in range(NH - 1):
            total = total + h_in[i, j] * h_scales[1 + j]
        rows = slice(i * QC, (i + 1) * QC)
        zt[1, rows, :] = total
        part = zt.at[1, pl.ds(i * QC, QC)]
        return [send(part, zt.at[b, pl.ds(i * QC, QC)], who) for b, who in zip((0, 2), y_peer)]

    f = [one for i in range(PARTS) for one in to_bands(i)]

    zq = nt(choose, zt[1])
    qa = nn(zq, wq_all) + cq_all
    qz = qa[:, 0:PATCH]
    qb = qa[:, PATCH:PATCH + 1]
    for one in f:
        one.wait_recv()
    logits = jnp.concatenate([nn(qz, zt[b]) for b in range(3)], axis=1) + qb
    same = q_ids == jnp.concatenate(id_rows, axis=1)
    logits = jnp.where(same, logits, -jnp.inf)
    attend = jnp.exp(logits - jnp.max(logits, axis=1, keepdims=True))
    attend = attend / jnp.sum(attend, axis=1, keepdims=True)
    zmix = sum(nt(attend[:, b * BAND:(b + 1) * BAND], zt[b]) for b in range(3))
    resid = (nn(zq, pv) + bv) + (nn(zmix, pval) + bval)
    center = jnp.mean(resid, axis=-1, keepdims=True)
    var = jnp.mean((resid - center) ** 2, axis=-1, keepdims=True)
    normed = (resid - center) / jnp.sqrt(var + 1e-05) * gain[...]
    hidden = jax.nn.gelu(nn(normed, up[...]) + upb[...])
    fin_out[...] = resid + nn(hidden, down[...])

    g = []
    for d in range(1, NX):
        rows = pl.ds(pl.multiple_of((c * NX + xs[d - 1]) * ROWS, ROWS), ROWS)
        g.append(send(fin_out.at[rows], fin_in.at[mine], x_peer[d - 1]))
    for d in range(NX):
        rows = pl.ds(pl.multiple_of(((1 - c) * NX + (x + d) % NX) * ROWS, ROWS), ROWS)
        g.append(send(fin_out.at[rows], fin_in.at[mine], sib if d == 0 else o_peer[d - 1]))
    fin_in[mine] = fin_out[pl.ds(pl.multiple_of(mine * ROWS, ROWS), ROWS)]
    for one in g:
        one.wait_recv()
    for k in range(K):
        out[:, k, :] = fin_in[k]
    for one in sends:
        one.wait_send()


COPIES = 90


def local(
    source_feat, target_feat, target_order, window_id, latent_query, patch_weight, patch_embed_bias, key_weight,
    value_matrix, window_query, window_key, window_value, window_out, norm_gain, up_weight, up_bias, down_weight,
):
    bands = lax.axis_size("src")
    tiles = target_feat.reshape(TARGETS // 8, 8, 2, 128).transpose(0, 2, 1, 3).reshape(2 * TARGETS, 128)
    params = (
        source_feat, target_order.reshape(32, 128), window_id.reshape(16, 128),
        latent_query, patch_weight, patch_embed_bias.reshape(1, -1), key_weight, value_matrix, window_query, window_key,
        window_value, window_out, norm_gain.reshape(1, -1), up_weight, up_bias.reshape(1, -1), down_weight,
    )
    vmem = pl.BlockSpec(memory_space=pltpu.VMEM)
    hbm = pl.BlockSpec(memory_space=pl.ANY)
    scratch = [pltpu.VMEM(p.shape, p.dtype) for p in params]
    scratch += [
        pltpu.VMEM((2 * TARGETS + 16, 128), F32),
        pltpu.VMEM((32, 128), jnp.int32),
        pltpu.SMEM((32, 128), jnp.int32),
        pltpu.VMEM((PATCHES, 8, 8, C), F32),
        pltpu.VMEM((NH, PIX, C), F32),
        pltpu.VMEM((BAND, 3 * C), jnp.bfloat16),
        pltpu.VMEM((PATCHES * K, C), F32),
        pltpu.VMEM((PATCHES, K, BAND), F32),
        pltpu.VMEM((PARTS, PATCHES, QC, BAND), F32),
        pltpu.VMEM((2, K, BAND), F32),
        pltpu.VMEM((2, K, BAND), F32),
        pltpu.VMEM((2, K, BAND), F32),
        pltpu.VMEM((K + NX - 1, 8, BAND), F32),
        pltpu.VMEM((NH, 8, BAND), F32),
        pltpu.VMEM((PARTS, K, QC, BAND), F32),
        pltpu.VMEM((PARTS, NX, QC, BAND), F32),
        pltpu.VMEM((PARTS, NX, QC, BAND), F32),
        pltpu.VMEM((PARTS, NX - 1, QC, BAND), F32),
        pltpu.VMEM((PARTS, QC, BAND), F32),
        pltpu.VMEM((PARTS, NH - 1, QC, BAND), F32),
        pltpu.VMEM((3, PATCH, BAND), F32),
        pltpu.VMEM((PIX, D), F32),
        pltpu.VMEM((K, ROWS, D), F32),
        pltpu.SemaphoreType.DMA((len(params),)),
        pltpu.SemaphoreType.DMA,
        pltpu.SemaphoreType.DMA,
        pltpu.SemaphoreType.DMA((COPIES,)),
        pltpu.SemaphoreType.DMA((COPIES,)),
    ]
    return pl.pallas_call(
        functools.partial(kernel, bands),
        out_shape=jax.ShapeDtypeStruct((ROWS, K, D), F32),
        in_specs=[hbm] * (1 + len(params)),
        out_specs=vmem,
        scratch_shapes=scratch,
        compiler_params=pltpu.CompilerParams(
            collective_id=0, has_side_effects=True, vmem_limit_bytes=60 * 1024 * 1024
        ),
        name="encode",
    )(tiles, *params)


def solution(mesh):
    placed = (P(("src", "tgt"), None), P("tgt", None), P("tgt")) + (P(),) * 14
    return jax.shard_map(
        local, mesh=mesh, in_specs=placed, out_specs=P(("src", "tgt"), None, None), check_vma=False
    )
```

```python
import functools
import math

import jax
import jax.numpy as jnp
from jax import lax
from jax.experimental import pallas as pl
from jax.experimental.pallas import tpu as pltpu
from jax.sharding import PartitionSpec as P

HI = lax.Precision.HIGHEST
MESH = pl.DeviceIdType.MESH
F32 = jnp.float32

NX, NH, NC = 4, 4, 2
BAND = 256
C = 256
D = 128
K = 8
PATCH = 64
TARGETS = 4096
PATCHES = TARGETS // PATCH
ROWS = 8
PARTS = 4
QC = PATCH // PARTS
SHRINK = 1.0 / math.sqrt(C)
PIX = BAND // NH


def nn(a, b):
    return lax.dot_general(a, b, (((1,), (0,)), ((), ())), precision=HI, preferred_element_type=F32)


def nt16(a, b):
    return lax.dot_general(a, b, (((1,), (1,)), ((), ())), preferred_element_type=F32)


def halves(a):
    high = a.astype(jnp.bfloat16)
    return high, (a - high.astype(F32)).astype(jnp.bfloat16)


def nn3(a, cat):
    high, low = halves(a)
    three = jnp.concatenate([high, high, low], axis=1)
    return lax.dot_general(three, cat, (((1,), (0,)), ((), ())), preferred_element_type=F32)


def nt(a, b):
    return lax.dot_general(a, b, (((1,), (1,)), ((), ())), precision=HI, preferred_element_type=F32)


def kernel(
    bands, tgt, src_h, order_h, wid_h, lq_h, pw_h, pb_h, kw_h, vm_h, wq_h, wk_h, wv_h, wo_h, gain_h, up_h, upb_h, down_h,
    out,
    order, wid, lq, pw, pb, kw, vm, wq, wk, wv, wo, gain, up, upb, down,
    raw, addr_v, addr, ordered, sbuf, scat, gmat, wts, cost,
    st, st_core, fac, st_x, st_h, zc, core_in, zx, x_in, zh, h_in, zt, up_cat, down_cat, fin_out, fin_in,
    wsem, tsem, asem, ksem, ssem, rsem,
):
    band = lax.axis_index("src")
    t = lax.axis_index("tgt")
    x = t // (NH * NC)
    h = (t // NC) % NH
    c = t % NC
    mine = c * NX + x

    def tid(xx, hh, cc):
        return (xx * NH + hh) * NC + cc

    sib = (band, tid(x, h, 1 - c))
    xs = [(x + d) % NX for d in range(1, NX)]
    hs = [(h + d) % NH for d in range(1, NH)]
    x_peer = [(band, tid(xx, h, c)) for xx in xs]
    h_peer = [(band, tid(x, hh, c)) for hh in hs]
    o_peer = [(band, tid((x + d) % NX, h, 1 - c)) for d in range(1, NX)]
    up_band = (band + 1) % bands
    down_band = (band + bands - 1) % bands
    y_peer = [(up_band, t), (down_band, t)]

    weights = list(zip(
        (order_h, wid_h, lq_h, pw_h, pb_h, kw_h, vm_h, wq_h, wk_h, wv_h, wo_h, gain_h, up_h, upb_h, down_h),
        (order, wid, lq, pw, pb, kw, vm, wq, wk, wv, wo, gain, up, upb, down),
    ))
    barrier = pltpu.get_barrier_semaphore()
    partners = h_peer + y_peer + x_peer + o_peer + [sib]
    for who in partners:
        pl.semaphore_signal(barrier, inc=1, device_id=who, device_id_type=MESH)
    loads = [pltpu.make_async_copy(a, b, wsem.at[i]) for i, (a, b) in enumerate(weights)]
    loads[0].start()
    load_target = pltpu.make_async_copy(tgt, raw.at[pl.ds(8, 2 * TARGETS)], tsem)
    load_target.start()
    slot = pl.multiple_of(c * (NX * ROWS) + x * ROWS, ROWS)
    half = pl.multiple_of(c * (NX * ROWS), NX * ROWS)
    own = sbuf.at[h, pl.ds(slot, ROWS)]
    keep = pltpu.make_async_copy(src_h, own, ksem)
    keep.start()

    count = [0]
    sends = []

    def send(a, b, who):
        n = count[0]
        count[0] = n + 1
        copy = pltpu.make_async_remote_copy(
            src_ref=a, dst_ref=b, send_sem=ssem.at[n], recv_sem=rsem.at[n], device_id=who, device_id_type=MESH
        )
        copy.start()
        sends.append(copy)
        return copy

    pl.semaphore_wait(barrier, len(partners))
    s1 = [send(src_h, own, who) for who in h_peer]
    for one in loads[1:]:
        one.start()

    loads[0].wait()
    ids = order[...] & (TARGETS - 1)
    addr_v[...] = (ids >> 3) * 16 + (ids & 7)
    to_smem = pltpu.make_async_copy(addr_v, addr, asem)
    to_smem.start()
    load_target.wait()
    to_smem.wait()
    sub = lax.broadcasted_iota(jnp.int32, (8, 128), 0)
    masks = [sub == i for i in range(8)]

    def gather_pair(r, _):
        for g in range(16):
            p = 2 * r + g // 8
            at = [addr[r, g * 8 + i] for i in range(8)]
            for lane in range(2):
                cols = slice(lane * 128, lane * 128 + 128)
                rows = [raw[pl.ds(at[i] + 8 + 8 * lane - i, 8), :] for i in range(8)]
                total = rows[0]
                for i in range(1, 8):
                    total = jnp.where(masks[i], rows[i], total)
                ordered[p, g % 8, :, cols] = total
        return 0

    lax.fori_loop(0, PATCHES // 2, gather_pair, 0)
    for one in loads[1:]:
        one.wait()
    scale = 1.0 / math.sqrt(D)
    kq = nt(lq[...], kw[...]) * scale
    w2 = nt(kq, pw[...]) * SHRINK
    bias_k = jnp.sum(kq * pb[...], axis=1, keepdims=True)
    w2x4 = jnp.concatenate([w2] * 4, axis=1)
    patch_of = lax.broadcasted_iota(jnp.int32, (K, 4 * PATCH), 1) // PATCH
    spread = jnp.concatenate([jnp.where(patch_of == i, w2x4, 0.0) for i in range(4)], axis=0)
    for one in s1:
        one.wait_recv()
    keep.wait()
    col = sbuf.at[:, pl.ds(slot, ROWS)]
    s2 = [send(col, col, who) for who in x_peer + o_peer + [sib]]

    def score_weights(g, _):
        block = ordered[pl.ds(g * 4, 4)].reshape(4 * PATCH, C)
        gmat[pl.ds(pl.multiple_of(g * 32, 32), 32), :] = nn(spread, block)
        return 0

    lax.fori_loop(0, PATCHES // 4, score_weights, 0, unroll=True)
    for one in s2:
        one.wait_recv()

    score = nt(gmat[...], sbuf[...].reshape(BAND, C)).reshape(PATCHES, K, BAND) + bias_k[None]
    peak = jnp.max(score, axis=0)
    weight = jnp.exp(score - peak[None])
    wts[...] = weight
    total = jnp.sum(weight, axis=0)
    st[0] = peak
    st[1] = total
    m1 = send(st, st_core, sib)

    shigh, slow = halves(sbuf[...].reshape(BAND, C) * SHRINK)
    scat[:, 0:C] = shigh
    scat[:, C:2 * C] = slow
    scat[:, 2 * C:3 * C] = shigh

    def cost_chunk(q):
        block = ordered[:, q * (QC // 8):(q + 1) * (QC // 8)].reshape(PATCHES * QC, C)
        a, b = halves(block)
        part = nt16(jnp.concatenate([a, a, b], axis=1), scat[...])
        cost[q] = part.reshape(PATCHES, QC, BAND)

    def join(values):
        top = functools.reduce(jnp.maximum, [a for a, _ in values])
        scales = [jnp.exp(a - top) for a, _ in values]
        return top, sum(b * f for (_, b), f in zip(values, scales)), scales

    cost_chunk(0)
    m1.wait_recv()
    top, tot, scales = join([(st[0], st[1]), (st_core[0], st_core[1])])
    fac[0] = scales[0]
    fac[1] = scales[1]
    for k in range(K):
        st_x[k, 0:1, :] = top[k:k + 1]
        st_x[k, 1:2, :] = tot[k:k + 1]
    m2 = [send(st_x.at[c * NX + xx], st_x.at[K + i], who) for i, (xx, who) in enumerate(zip(xs, x_peer))]

    def sums(i):
        for lane in range(2):
            cols = slice(lane * 128, lane * 128 + 128)

            def step(p, acc):
                rows = [cost[i, p, g * 8:g * 8 + 8, cols] for g in range(QC // 8)]
                new = []
                for k in range(K):
                    w = jnp.broadcast_to(wts[p, k:k + 1, cols], (8, 128))
                    new.extend(acc[k * len(rows) + g] + w * one for g, one in enumerate(rows))
                return tuple(new)

            zero = tuple(jnp.zeros((8, 128), F32) for _ in range(QC // 8 * K))
            acc = lax.fori_loop(0, PATCHES, step, zero, unroll=True)
            for k in range(K):
                for g in range(QC // 8):
                    zc[i, k, g * 8:g * 8 + 8, cols] = acc[k * (QC // 8) + g]
        return send(zc.at[i, pl.ds((1 - c) * NX, NX)], core_in.at[i], sib)

    def over_x(i, came):
        came.wait_recv()
        for j in range(NX):
            k = c * NX + j
            zx[i, j] = zc[i, k] * fac[0, pl.ds(k, 1), :] + core_in[i, j] * fac[1, pl.ds(k, 1), :]
        return [send(zx.at[i, xx], x_in.at[i, j], who) for j, (xx, who) in enumerate(zip(xs, x_peer))]

    def x_stats():
        for one in m2:
            one.wait_recv()
        top, tot, scales = join([(st_x[i, 0:1, :], st_x[i, 1:2, :]) for i in (mine, K, K + 1, K + 2)])
        st_h[0, 0:1, :] = top
        st_h[0, 1:2, :] = tot
        return [send(st_h.at[0], st_h.at[1 + i], who) for i, who in enumerate(h_peer)], scales

    cost_chunk(1)
    core = [sums(0)]
    over = []
    for i in range(1, PARTS):
        if i + 1 < PARTS:
            cost_chunk(i + 1)
        core.append(sums(i))
        over.append(over_x(i - 1, core[i - 1]))
    over.append(over_x(PARTS - 1, core[PARTS - 1]))
    m3, x_scales = x_stats()

    def over_h(i, came):
        for one in came:
            one.wait_recv()
        total = zx[i, x] * x_scales[0]
        for j in range(NX - 1):
            total = total + x_in[i, j] * x_scales[1 + j]
        zh[i] = total
        return [send(zh.at[i], h_in.at[i, j], who) for j, who in enumerate(h_peer)]

    d = [over_h(i, came) for i, came in enumerate(over)]
    pv = nn(pw[...], vm[...])
    bv = nn(pb[...], vm[...])
    pk = nn(pv, wk[...])
    bk = nn(bv, wk[...])
    pq = nn(pv, wq[...]) * scale
    bq = nn(bv, wq[...]) * scale
    val = nn(wv[...], wo[...])
    pval = nn(pv, val)
    bval = nn(bv, val)
    pk_all = jnp.concatenate([pk, jnp.broadcast_to(bk, (PATCH, D))], axis=0)
    wq_all = nt(pq, pk_all)
    cq_all = nt(bq, pk_all)

    nat = lax.broadcasted_iota(jnp.int32, (BAND, BAND), 0)
    pos = lax.broadcasted_iota(jnp.int32, (BAND, BAND), 1)
    ph, pc, px, pr = pos // 64, (pos // 32) % 2, (pos // 8) % 4, pos % 8
    perm = jnp.where(nat == px * 64 + ph * 16 + pc * 8 + pr, 1.0, 0.0).astype(F32)
    id_rows = []
    for b in (down_band, band, up_band):
        two = [wid[pl.ds(2 * b + i, 1), :].astype(F32) for i in range(2)]
        id_rows.append(nn(jnp.broadcast_to(jnp.concatenate(two, axis=1), (8, BAND)), perm)[0:1])
    picked = lax.broadcasted_iota(jnp.int32, (PIX, BAND), 1) == lax.broadcasted_iota(jnp.int32, (PIX, BAND), 0) + h * PIX
    q_ids = jnp.sum(jnp.where(picked, id_rows[1], 0.0), axis=1, keepdims=True)
    choose = jnp.where(picked, 1.0, 0.0).astype(F32)

    for ref, cat in ((up, up_cat), (down, down_cat)):
        n = ref.shape[0]
        a, b = halves(ref[...])
        cat[0:n, :] = a
        cat[n:2 * n, :] = b
        cat[2 * n:3 * n, :] = a
    for one in m3:
        one.wait_recv()
    _, tot, h_scales = join([(st_h[i, 0:1, :], st_h[i, 1:2, :]) for i in range(NH)])
    inverse = 1.0 / tot
    h_scales = [f * inverse for f in h_scales]

    def to_bands(i):
        for one in d[i]:
            one.wait_recv()
        total = zh[i] * h_scales[0]
        for j in range(NH - 1):
            total = total + h_in[i, j] * h_scales[1 + j]
        rows = slice(i * QC, (i + 1) * QC)
        zt[1, rows, :] = total
        part = zt.at[1, pl.ds(i * QC, QC)]
        return [send(part, zt.at[b, pl.ds(i * QC, QC)], who) for b, who in zip((0, 2), y_peer)]

    f = [one for i in range(PARTS) for one in to_bands(i)]

    zq = nt(choose, zt[1])
    qa = nn(zq, wq_all) + cq_all
    qz = qa[:, 0:PATCH]
    qb = qa[:, PATCH:PATCH + 1]
    middle = nn(qz, zt[1])
    for one in f:
        one.wait_recv()
    logits = jnp.concatenate([nn(qz, zt[0]), middle, nn(qz, zt[2])], axis=1) + qb
    same = q_ids == jnp.concatenate(id_rows, axis=1)
    logits = jnp.where(same, logits, -jnp.inf)
    attend = jnp.exp(logits - jnp.max(logits, axis=1, keepdims=True))
    attend = attend / jnp.sum(attend, axis=1, keepdims=True)
    zmix = sum(nt(attend[:, b * BAND:(b + 1) * BAND], zt[b]) for b in range(3))
    resid = (nn(zq, pv) + bv) + (nn(zmix, pval) + bval)
    center = jnp.mean(resid, axis=-1, keepdims=True)
    var = jnp.mean((resid - center) ** 2, axis=-1, keepdims=True)
    normed = (resid - center) / jnp.sqrt(var + 1e-05) * gain[...]
    hidden = jax.nn.gelu(nn3(normed, up_cat[...]) + upb[...])
    fin_out[...] = resid + nn3(hidden, down_cat[...])

    early = len(sends)
    g = []
    for i, cc in ((1, 1 - c), (2, 1 - c), (3, 1 - c), (1, c), (2, c), (3, c), (0, 1 - c)):
        rows = pl.ds(pl.multiple_of((cc * NX + (x + i) % NX) * ROWS, ROWS), ROWS)
        g.append(send(fin_out.at[rows], fin_in.at[mine], (band, tid((x + i) % NX, h, cc))))
    for one in sends[:early]:
        one.wait_send()
    fin_in[mine] = fin_out[pl.ds(pl.multiple_of(mine * ROWS, ROWS), ROWS)]
    for one in g:
        one.wait_recv()
    for k in range(K):
        out[:, k, :] = fin_in[k]
    for one in g:
        one.wait_send()


COPIES = 90


def local(
    source_feat, target_feat, target_order, window_id, latent_query, patch_weight, patch_embed_bias, key_weight,
    value_matrix, window_query, window_key, window_value, window_out, norm_gain, up_weight, up_bias, down_weight,
):
    bands = lax.axis_size("src")
    tiles = target_feat.reshape(TARGETS // 8, 8, 2, 128).transpose(0, 2, 1, 3).reshape(2 * TARGETS, 128)
    params = (
        target_order.reshape(32, 128), window_id.reshape(16, 128),
        latent_query, patch_weight, patch_embed_bias.reshape(1, -1), key_weight, value_matrix, window_query, window_key,
        window_value, window_out, norm_gain.reshape(1, -1), up_weight, up_bias.reshape(1, -1), down_weight,
    )
    vmem = pl.BlockSpec(memory_space=pltpu.VMEM)
    hbm = pl.BlockSpec(memory_space=pl.ANY)
    scratch = [pltpu.VMEM(p.shape, p.dtype) for p in params]
    scratch += [
        pltpu.VMEM((2 * TARGETS + 16, 128), F32),
        pltpu.VMEM((32, 128), jnp.int32),
        pltpu.SMEM((32, 128), jnp.int32),
        pltpu.VMEM((PATCHES, 8, 8, C), F32),
        pltpu.VMEM((NH, PIX, C), F32),
        pltpu.VMEM((BAND, 3 * C), jnp.bfloat16),
        pltpu.VMEM((PATCHES * K, C), F32),
        pltpu.VMEM((PATCHES, K, BAND), F32),
        pltpu.VMEM((PARTS, PATCHES, QC, BAND), F32),
        pltpu.VMEM((2, K, BAND), F32),
        pltpu.VMEM((2, K, BAND), F32),
        pltpu.VMEM((2, K, BAND), F32),
        pltpu.VMEM((K + NX - 1, 8, BAND), F32),
        pltpu.VMEM((NH, 8, BAND), F32),
        pltpu.VMEM((PARTS, K, QC, BAND), F32),
        pltpu.VMEM((PARTS, NX, QC, BAND), F32),
        pltpu.VMEM((PARTS, NX, QC, BAND), F32),
        pltpu.VMEM((PARTS, NX - 1, QC, BAND), F32),
        pltpu.VMEM((PARTS, QC, BAND), F32),
        pltpu.VMEM((PARTS, NH - 1, QC, BAND), F32),
        pltpu.VMEM((3, PATCH, BAND), F32),
        pltpu.VMEM((3 * D, 512), jnp.bfloat16),
        pltpu.VMEM((3 * 512, D), jnp.bfloat16),
        pltpu.VMEM((PIX, D), F32),
        pltpu.VMEM((K, ROWS, D), F32),
        pltpu.SemaphoreType.DMA((len(params),)),
        pltpu.SemaphoreType.DMA,
        pltpu.SemaphoreType.DMA,
        pltpu.SemaphoreType.DMA,
        pltpu.SemaphoreType.DMA((COPIES,)),
        pltpu.SemaphoreType.DMA((COPIES,)),
    ]
    return pl.pallas_call(
        functools.partial(kernel, bands),
        out_shape=jax.ShapeDtypeStruct((ROWS, K, D), F32),
        in_specs=[hbm] * (2 + len(params)),
        out_specs=vmem,
        scratch_shapes=scratch,
        compiler_params=pltpu.CompilerParams(
            collective_id=0, has_side_effects=True, vmem_limit_bytes=60 * 1024 * 1024
        ),
        name="encode",
    )(tiles, source_feat, *params)


def solution(mesh):
    placed = (P(("src", "tgt"), None), P("tgt", None), P("tgt")) + (P(),) * 14
    return jax.shard_map(
        local, mesh=mesh, in_specs=placed, out_specs=P(("src", "tgt"), None, None), check_vma=False
    )
```

```python
import functools
import math

import jax
import jax.numpy as jnp
from jax import lax
from jax.experimental import pallas as pl
from jax.experimental.pallas import tpu as pltpu
from jax.sharding import PartitionSpec as P

HI = lax.Precision.HIGHEST
MESH = pl.DeviceIdType.MESH
F32 = jnp.float32

NX, NH, NC = 4, 4, 2
BAND = 256
C = 256
D = 128
K = 8
PATCH = 64
TARGETS = 4096
PATCHES = TARGETS // PATCH
ROWS = 8
PARTS = 4
QC = PATCH // PARTS
SHRINK = 1.0 / math.sqrt(C)
PIX = BAND // NH


def nn(a, b):
    return lax.dot_general(a, b, (((1,), (0,)), ((), ())), precision=HI, preferred_element_type=F32)


def nt16(a, b):
    return lax.dot_general(a, b, (((1,), (1,)), ((), ())), preferred_element_type=F32)


def halves(a):
    high = a.astype(jnp.bfloat16)
    return high, (a - high.astype(F32)).astype(jnp.bfloat16)


def nn3(a, cat):
    high, low = halves(a)
    three = jnp.concatenate([high, high, low], axis=1)
    return lax.dot_general(three, cat, (((1,), (0,)), ((), ())), preferred_element_type=F32)


def nt(a, b):
    return lax.dot_general(a, b, (((1,), (1,)), ((), ())), precision=HI, preferred_element_type=F32)


def kernel(
    bands, tgt, src_h, order_h, wid_h, lq_h, pw_h, pb_h, kw_h, vm_h, wq_h, wk_h, wv_h, wo_h, gain_h, up_h, upb_h, down_h,
    out,
    order, wid, lq, pw, pb, kw, vm, wq, wk, wv, wo, gain, up, upb, down,
    raw, addr_v, addr, ordered, sbuf, scat, gmat, wts, cost,
    st, st_core, fac, st_x, st_h, zc, core_in, zx, x_in, zh, h_in, zt, up_cat, down_cat, fin_out, fin_in,
    wsem, tsem, asem, ksem, ssem, rsem,
):
    band = lax.axis_index("src")
    t = lax.axis_index("tgt")
    x = t // (NH * NC)
    h = (t // NC) % NH
    c = t % NC
    mine = c * NX + x

    def tid(xx, hh, cc):
        return (xx * NH + hh) * NC + cc

    sib = (band, tid(x, h, 1 - c))
    xs = [(x + d) % NX for d in (2, 1, 3)]
    hs = [(h + d) % NH for d in (2, 1, 3)]
    x_peer = [(band, tid(xx, h, c)) for xx in xs]
    h_peer = [(band, tid(x, hh, c)) for hh in hs]
    o_peer = [(band, tid((x + d) % NX, h, 1 - c)) for d in range(1, NX)]
    up_band = (band + 1) % bands
    down_band = (band + bands - 1) % bands
    y_peer = [(up_band, t), (down_band, t)]

    weights = list(zip(
        (order_h, wid_h, lq_h, pw_h, pb_h, kw_h, vm_h, wq_h, wk_h, wv_h, wo_h, gain_h, up_h, upb_h, down_h),
        (order, wid, lq, pw, pb, kw, vm, wq, wk, wv, wo, gain, up, upb, down),
    ))
    barrier = pltpu.get_barrier_semaphore()
    partners = h_peer + y_peer + x_peer + o_peer + [sib]
    for who in partners:
        pl.semaphore_signal(barrier, inc=1, device_id=who, device_id_type=MESH)
    loads = [pltpu.make_async_copy(a, b, wsem.at[i]) for i, (a, b) in enumerate(weights)]
    loads[0].start()
    load_target = pltpu.make_async_copy(tgt, raw.at[pl.ds(8, 2 * TARGETS)], tsem)
    load_target.start()
    slot = pl.multiple_of(c * (NX * ROWS) + x * ROWS, ROWS)
    half = pl.multiple_of(c * (NX * ROWS), NX * ROWS)
    own = sbuf.at[h, pl.ds(slot, ROWS)]
    keep = pltpu.make_async_copy(src_h, own, ksem)
    keep.start()

    count = [0]
    sends = []

    def send(a, b, who):
        n = count[0]
        count[0] = n + 1
        copy = pltpu.make_async_remote_copy(
            src_ref=a, dst_ref=b, send_sem=ssem.at[n], recv_sem=rsem.at[n], device_id=who, device_id_type=MESH
        )
        copy.start()
        sends.append(copy)
        return copy

    pl.semaphore_wait(barrier, len(partners))
    s1 = [send(src_h, own, who) for who in h_peer]
    for one in loads[1:]:
        one.start()

    loads[0].wait()
    ids = order[...] & (TARGETS - 1)
    addr_v[...] = (ids >> 3) * 16 + (ids & 7)
    to_smem = pltpu.make_async_copy(addr_v, addr, asem)
    to_smem.start()
    load_target.wait()
    to_smem.wait()
    sub = lax.broadcasted_iota(jnp.int32, (8, 128), 0)
    masks = [sub == i for i in range(8)]

    def gather_pair(r, _):
        for g in range(16):
            p = 2 * r + g // 8
            at = [addr[r, g * 8 + i] for i in range(8)]
            for lane in range(2):
                cols = slice(lane * 128, lane * 128 + 128)
                rows = [raw[pl.ds(at[i] + 8 + 8 * lane - i, 8), :] for i in range(8)]
                total = rows[0]
                for i in range(1, 8):
                    total = jnp.where(masks[i], rows[i], total)
                ordered[p, g % 8, :, cols] = total
        return 0

    lax.fori_loop(0, PATCHES // 2, gather_pair, 0)
    for one in loads[1:]:
        one.wait()
    scale = 1.0 / math.sqrt(D)
    kq = nt(lq[...], kw[...]) * scale
    w2 = nt(kq, pw[...]) * SHRINK
    bias_k = jnp.sum(kq * pb[...], axis=1, keepdims=True)
    w2x4 = jnp.concatenate([w2] * 4, axis=1)
    patch_of = lax.broadcasted_iota(jnp.int32, (K, 4 * PATCH), 1) // PATCH
    spread = jnp.concatenate([jnp.where(patch_of == i, w2x4, 0.0) for i in range(4)], axis=0)
    for one in s1:
        one.wait_recv()
    keep.wait()
    col = sbuf.at[:, pl.ds(slot, ROWS)]
    s2 = [send(col, col, who) for who in x_peer + o_peer + [sib]]

    def score_weights(g, _):
        block = ordered[pl.ds(g * 4, 4)].reshape(4 * PATCH, C)
        gmat[pl.ds(pl.multiple_of(g * 32, 32), 32), :] = nn(spread, block)
        return 0

    lax.fori_loop(0, PATCHES // 4, score_weights, 0, unroll=True)
    for one in s2:
        one.wait_recv()

    score = nt(gmat[...], sbuf[...].reshape(BAND, C)).reshape(PATCHES, K, BAND) + bias_k[None]
    peak = jnp.max(score, axis=0)
    weight = jnp.exp(score - peak[None])
    wts[...] = weight
    total = jnp.sum(weight, axis=0)
    st[0] = peak
    st[1] = total
    m1 = send(st, st_core, sib)

    shigh, slow = halves(sbuf[...].reshape(BAND, C) * SHRINK)
    scat[:, 0:C] = shigh
    scat[:, C:2 * C] = slow
    scat[:, 2 * C:3 * C] = shigh

    def cost_chunk(q):
        block = ordered[:, q * (QC // 8):(q + 1) * (QC // 8)].reshape(PATCHES * QC, C)
        a, b = halves(block)
        part = nt16(jnp.concatenate([a, a, b], axis=1), scat[...])
        cost[q] = part.reshape(PATCHES, QC, BAND)

    def join(values):
        top = functools.reduce(jnp.maximum, [a for a, _ in values])
        scales = [jnp.exp(a - top) for a, _ in values]
        return top, sum(b * f for (_, b), f in zip(values, scales)), scales

    cost_chunk(0)
    m1.wait_recv()
    top, tot, scales = join([(st[0], st[1]), (st_core[0], st_core[1])])
    fac[0] = scales[0]
    fac[1] = scales[1]
    for k in range(K):
        st_x[k, 0:1, :] = top[k:k + 1]
        st_x[k, 1:2, :] = tot[k:k + 1]
    m2 = [send(st_x.at[c * NX + xx], st_x.at[K + i], who) for i, (xx, who) in enumerate(zip(xs, x_peer))]

    def sums(i):
        for lane in range(2):
            cols = slice(lane * 128, lane * 128 + 128)

            def step(p, acc):
                rows = [cost[i, p, g * 8:g * 8 + 8, cols] for g in range(QC // 8)]
                new = []
                for k in range(K):
                    w = jnp.broadcast_to(wts[p, k:k + 1, cols], (8, 128))
                    new.extend(acc[k * len(rows) + g] + w * one for g, one in enumerate(rows))
                return tuple(new)

            zero = tuple(jnp.zeros((8, 128), F32) for _ in range(QC // 8 * K))
            acc = lax.fori_loop(0, PATCHES, step, zero, unroll=True)
            for k in range(K):
                for g in range(QC // 8):
                    zc[i, k, g * 8:g * 8 + 8, cols] = acc[k * (QC // 8) + g]
        return send(zc.at[i, pl.ds((1 - c) * NX, NX)], core_in.at[i], sib)

    def over_x(i, came):
        came.wait_recv()
        for j in range(NX):
            k = c * NX + j
            zx[i, j] = zc[i, k] * fac[0, pl.ds(k, 1), :] + core_in[i, j] * fac[1, pl.ds(k, 1), :]
        return [send(zx.at[i, xx], x_in.at[i, j], who) for j, (xx, who) in enumerate(zip(xs, x_peer))]

    def x_stats():
        for one in m2:
            one.wait_recv()
        top, tot, scales = join([(st_x[i, 0:1, :], st_x[i, 1:2, :]) for i in (mine, K, K + 1, K + 2)])
        st_h[0, 0:1, :] = top
        st_h[0, 1:2, :] = tot
        return [send(st_h.at[0], st_h.at[1 + i], who) for i, who in enumerate(h_peer)], scales

    cost_chunk(1)
    core = [sums(0)]
    over = []
    for i in range(1, PARTS):
        if i + 1 < PARTS:
            cost_chunk(i + 1)
        core.append(sums(i))
        over.append(over_x(i - 1, core[i - 1]))
    over.append(over_x(PARTS - 1, core[PARTS - 1]))
    m3, x_scales = x_stats()

    def over_h(i, came):
        for one in came:
            one.wait_recv()
        total = zx[i, x] * x_scales[0]
        for j in range(NX - 1):
            total = total + x_in[i, j] * x_scales[1 + j]
        zh[i] = total
        return [send(zh.at[i], h_in.at[i, j], who) for j, who in enumerate(h_peer)]

    d = [over_h(i, came) for i, came in enumerate(over)]
    pv = nn(pw[...], vm[...])
    bv = nn(pb[...], vm[...])
    pk = nn(pv, wk[...])
    bk = nn(bv, wk[...])
    pq = nn(pv, wq[...]) * scale
    bq = nn(bv, wq[...]) * scale
    val = nn(wv[...], wo[...])
    pval = nn(pv, val)
    bval = nn(bv, val)
    pk_all = jnp.concatenate([pk, jnp.broadcast_to(bk, (PATCH, D))], axis=0)
    wq_all = nt(pq, pk_all)
    cq_all = nt(bq, pk_all)

    nat = lax.broadcasted_iota(jnp.int32, (BAND, BAND), 0)
    pos = lax.broadcasted_iota(jnp.int32, (BAND, BAND), 1)
    ph, pc, px, pr = pos // 64, (pos // 32) % 2, (pos // 8) % 4, pos % 8
    perm = jnp.where(nat == px * 64 + ph * 16 + pc * 8 + pr, 1.0, 0.0).astype(F32)
    id_rows = []
    for b in (down_band, band, up_band):
        two = [wid[pl.ds(2 * b + i, 1), :].astype(F32) for i in range(2)]
        id_rows.append(nn(jnp.broadcast_to(jnp.concatenate(two, axis=1), (8, BAND)), perm)[0:1])
    picked = lax.broadcasted_iota(jnp.int32, (PIX, BAND), 1) == lax.broadcasted_iota(jnp.int32, (PIX, BAND), 0) + h * PIX
    q_ids = jnp.sum(jnp.where(picked, id_rows[1], 0.0), axis=1, keepdims=True)
    choose = jnp.where(picked, 1.0, 0.0).astype(F32)

    for ref, cat in ((up, up_cat), (down, down_cat)):
        n = ref.shape[0]
        a, b = halves(ref[...])
        cat[0:n, :] = a
        cat[n:2 * n, :] = b
        cat[2 * n:3 * n, :] = a
    for one in m3:
        one.wait_recv()
    _, tot, h_scales = join([(st_h[i, 0:1, :], st_h[i, 1:2, :]) for i in range(NH)])
    inverse = 1.0 / tot
    h_scales = [f * inverse for f in h_scales]

    def to_bands(i):
        for one in d[i]:
            one.wait_recv()
        total = zh[i] * h_scales[0]
        for j in range(NH - 1):
            total = total + h_in[i, j] * h_scales[1 + j]
        rows = slice(i * QC, (i + 1) * QC)
        zt[1, rows, :] = total
        part = zt.at[1, pl.ds(i * QC, QC)]
        return [send(part, zt.at[b, pl.ds(i * QC, QC)], who) for b, who in zip((0, 2), y_peer)]

    f = [one for i in range(PARTS) for one in to_bands(i)]

    zq = nt(choose, zt[1])
    qa = nn(zq, wq_all) + cq_all
    qz = qa[:, 0:PATCH]
    qb = qa[:, PATCH:PATCH + 1]
    middle = nn(qz, zt[1])
    for one in f:
        one.wait_recv()
    logits = jnp.concatenate([nn(qz, zt[0]), middle, nn(qz, zt[2])], axis=1) + qb
    same = q_ids == jnp.concatenate(id_rows, axis=1)
    logits = jnp.where(same, logits, -jnp.inf)
    attend = jnp.exp(logits - jnp.max(logits, axis=1, keepdims=True))
    attend = attend / jnp.sum(attend, axis=1, keepdims=True)
    zmix = sum(nt(attend[:, b * BAND:(b + 1) * BAND], zt[b]) for b in range(3))
    resid = (nn(zq, pv) + bv) + (nn(zmix, pval) + bval)
    center = jnp.mean(resid, axis=-1, keepdims=True)
    var = jnp.mean((resid - center) ** 2, axis=-1, keepdims=True)
    normed = (resid - center) / jnp.sqrt(var + 1e-05) * gain[...]
    hidden = jax.nn.gelu(nn3(normed, up_cat[...]) + upb[...])
    fin_out[...] = resid + nn3(hidden, down_cat[...])

    early = len(sends)
    g = []
    for i, cc in ((1, 1 - c), (2, 1 - c), (3, 1 - c), (1, c), (2, c), (3, c), (0, 1 - c)):
        rows = pl.ds(pl.multiple_of((cc * NX + (x + i) % NX) * ROWS, ROWS), ROWS)
        g.append(send(fin_out.at[rows], fin_in.at[mine], (band, tid((x + i) % NX, h, cc))))
    for one in sends[:early]:
        one.wait_send()
    fin_in[mine] = fin_out[pl.ds(pl.multiple_of(mine * ROWS, ROWS), ROWS)]
    for one in g:
        one.wait_recv()
    for k in range(K):
        out[:, k, :] = fin_in[k]
    for one in g:
        one.wait_send()


COPIES = 90


def local(
    source_feat, target_feat, target_order, window_id, latent_query, patch_weight, patch_embed_bias, key_weight,
    value_matrix, window_query, window_key, window_value, window_out, norm_gain, up_weight, up_bias, down_weight,
):
    bands = lax.axis_size("src")
    tiles = target_feat.reshape(TARGETS // 8, 8, 2, 128).transpose(0, 2, 1, 3).reshape(2 * TARGETS, 128)
    params = (
        target_order.reshape(32, 128), window_id.reshape(16, 128),
        latent_query, patch_weight, patch_embed_bias.reshape(1, -1), key_weight, value_matrix, window_query, window_key,
        window_value, window_out, norm_gain.reshape(1, -1), up_weight, up_bias.reshape(1, -1), down_weight,
    )
    vmem = pl.BlockSpec(memory_space=pltpu.VMEM)
    hbm = pl.BlockSpec(memory_space=pl.ANY)
    scratch = [pltpu.VMEM(p.shape, p.dtype) for p in params]
    scratch += [
        pltpu.VMEM((2 * TARGETS + 16, 128), F32),
        pltpu.VMEM((32, 128), jnp.int32),
        pltpu.SMEM((32, 128), jnp.int32),
        pltpu.VMEM((PATCHES, 8, 8, C), F32),
        pltpu.VMEM((NH, PIX, C), F32),
        pltpu.VMEM((BAND, 3 * C), jnp.bfloat16),
        pltpu.VMEM((PATCHES * K, C), F32),
        pltpu.VMEM((PATCHES, K, BAND), F32),
        pltpu.VMEM((PARTS, PATCHES, QC, BAND), F32),
        pltpu.VMEM((2, K, BAND), F32),
        pltpu.VMEM((2, K, BAND), F32),
        pltpu.VMEM((2, K, BAND), F32),
        pltpu.VMEM((K + NX - 1, 8, BAND), F32),
        pltpu.VMEM((NH, 8, BAND), F32),
        pltpu.VMEM((PARTS, K, QC, BAND), F32),
        pltpu.VMEM((PARTS, NX, QC, BAND), F32),
        pltpu.VMEM((PARTS, NX, QC, BAND), F32),
        pltpu.VMEM((PARTS, NX - 1, QC, BAND), F32),
        pltpu.VMEM((PARTS, QC, BAND), F32),
        pltpu.VMEM((PARTS, NH - 1, QC, BAND), F32),
        pltpu.VMEM((3, PATCH, BAND), F32),
        pltpu.VMEM((3 * D, 512), jnp.bfloat16),
        pltpu.VMEM((3 * 512, D), jnp.bfloat16),
        pltpu.VMEM((PIX, D), F32),
        pltpu.VMEM((K, ROWS, D), F32),
        pltpu.SemaphoreType.DMA((len(params),)),
        pltpu.SemaphoreType.DMA,
        pltpu.SemaphoreType.DMA,
        pltpu.SemaphoreType.DMA,
        pltpu.SemaphoreType.DMA((COPIES,)),
        pltpu.SemaphoreType.DMA((COPIES,)),
    ]
    return pl.pallas_call(
        functools.partial(kernel, bands),
        out_shape=jax.ShapeDtypeStruct((ROWS, K, D), F32),
        in_specs=[hbm] * (2 + len(params)),
        out_specs=vmem,
        scratch_shapes=scratch,
        compiler_params=pltpu.CompilerParams(
            collective_id=0, has_side_effects=True, vmem_limit_bytes=60 * 1024 * 1024
        ),
        name="encode",
    )(tiles, source_feat, *params)


def solution(mesh):
    placed = (P(("src", "tgt"), None), P("tgt", None), P("tgt")) + (P(),) * 14
    return jax.shard_map(
        local, mesh=mesh, in_specs=placed, out_specs=P(("src", "tgt"), None, None), check_vma=False
    )
```
